32 devices in a mesh: mesh: 8 (over z, x), sub: 4 (over y, core).
Axes of the slice: x: 2, y: 2, z: 4, core: 2. Of those that a mesh axis runs over, the one named last changes fastest.
Arguments:
- conductivity: float32 [4, 32, 2, 64, 128], P('sub', 'mesh'), may hold values from 0.3 to 3
- footprint: int32 [8, 8], replicated, may hold values from 0 to 31, as said below
- initial: float32 [8, 8, 512, 128], P('mesh', 'sub'), may hold values from -30 to 30
- observed: float32 [8, 3, 8, 512, 128], P('mesh', None, 'sub'), may hold values from -6 to 6
Outputs:
- gradient: float32 [4, 32, 2, 64, 128], P('sub', 'mesh')
- last_field: float32 [8, 8, 512, 128], P('mesh', 'sub')
The draws below stay inside these ranges and needn't reach their ends.
Inputs may be any that keep to these rules, and one draw needn't show every extreme that they name: `footprint`: each row names 8 different blocks; in every row, each range k * 4 to (k + 1) * 4 - 1 holds at most one of the row's ids.
All inputs are finite; a program needn't handle non-finite values.
Results may differ from the reference program's by a relative error of at most 0.00011.
Values sent between devices are 32-bit elements; how exact they have to be, the bound alone decides.
A program may use at most 128 MiB of HBM per device.

```python
import math
import jax
import jax.numpy as jnp
from jax import lax

CX = 2
BY = 64
CZ = 128
TILES = 8
BLK_DEV = 4
STEPS = 3
DEG = 6
NX = 8
NY = 512
NBLK = 32
N_MESH = 8
N_SUB = 4


def draw_footprint(key, part):
    first_key, third_key = jax.random.split(jax.random.fold_in(key, 7), 2)
    capacity = max(1, TILES // N_MESH)
    stride = max(1, N_MESH // TILES)
    owner_first = jax.random.randint(first_key, (N_MESH, 1), 0, N_MESH, dtype=jnp.int32)
    column = jnp.arange(TILES, dtype=jnp.int32)[None, :]
    owners = (owner_first + column % N_MESH * stride) % N_MESH
    cycle = column // N_MESH
    local_base = jax.random.randint(third_key, (N_MESH, TILES), 0, BLK_DEV // capacity, dtype=jnp.int32)
    local_ids = local_base * capacity + cycle
    return (owners * BLK_DEV + local_ids).astype(jnp.int32)


def level_of(key, extent, pieces, low, top_value):
    gain = 1.0
    for dim, parts in pieces:
        draws = jax.random.uniform(jax.random.fold_in(jax.random.fold_in(key, 6), dim), (parts,), jnp.float32, low / len(pieces), top_value / len(pieces))
        gain = gain * jnp.repeat(jnp.exp(draws), extent[dim] // parts).reshape((-1,) + (1,) * (len(extent) - 1 - dim))
    return gain


def centred(stream_key, extent, scale, most, pieces=(), kind=jnp.bfloat16):
    array = scale * jax.random.normal(stream_key, extent, jnp.float32)
    if pieces:
        array = array * level_of(stream_key, extent, pieces, -0.22, 0.18)
    return jnp.clip(array, -most, most).astype(kind)


def setup_inputs(seed: int = 0) -> dict:
    arg_keys = jax.random.split(jax.random.key(seed), 5)
    return {
        "conductivity": jnp.clip(jnp.exp(math.log(3.0) - 2.3025851 * jax.random.uniform(arg_keys[0], (N_SUB, NBLK, CX, BY, CZ), jnp.float32) ** level_of(arg_keys[0], (N_SUB, NBLK, CX, BY, CZ), ((0, 4), (1, 8)), -0.2, 0.2)), 0.3, 3.0),
        "footprint": draw_footprint(jax.random.fold_in(arg_keys[4], 71), 0),
        "initial": centred(arg_keys[2], (N_MESH, NX, NY, CZ), 5.0, 30.0, ((0, 8), (1, 4)), jnp.float32),
        "observed": centred(arg_keys[3], (N_MESH, STEPS, NX, NY, CZ), 1.0, 6.0, ((0, 8), (2, 4)), jnp.float32),
    }


low_bound = 0.3
high_bound = 15.0


def apply_operator(field, conduct):
    padded = jnp.pad(field, 1)
    beside = padded[2:, 1:-1, 1:-1] + padded[:-2, 1:-1, 1:-1]
    beside = beside + padded[1:-1, 2:, 1:-1] + padded[1:-1, :-2, 1:-1]
    beside = beside + padded[1:-1, 1:-1, 2:] + padded[1:-1, 1:-1, :-2]
    return (6.0 + conduct) * field - beside


def chebyshev(source, conduct, operate):
    centre = (high_bound + low_bound) / 2.0
    half_width = (high_bound - low_bound) / 2.0
    ratio_now = half_width / centre
    direct = source / centre
    remain = source
    iterate = direct
    for repeat in range(DEG):
        remain = remain - operate(direct, conduct)
        ratio_next = 1.0 / (2.0 * centre / half_width - ratio_now)
        direct = (ratio_next * ratio_now) * direct + (2.0 * ratio_next / half_width) * remain
        iterate = iterate + direct
        ratio_now = ratio_next
    return iterate


def one_mesh(conduct, start_field, observed_mesh, operate):
    fields = [start_field]
    for step in range(STEPS):
        fields.append(chebyshev(conduct * fields[-1], conduct, operate))
    adjoint = jnp.zeros_like(start_field)
    summed = jnp.zeros_like(start_field)
    for step in range(STEPS, 0, -1):
        adjoint = chebyshev(fields[step] - observed_mesh[step - 1] + conduct * adjoint, conduct, operate)
        summed = summed + adjoint * (fields[step - 1] - fields[step])
    return fields[-1], summed


def reference(conductivity, footprint, initial, observed):
    def per_mesh(carry, inputs):
        block_ids, start_field, observed_mesh = inputs
        picked = conductivity[:, block_ids]
        conduct = jnp.transpose(picked, (0, 2, 1, 3, 4)).reshape(N_SUB * CX, TILES * BY, CZ)
        final_field, summed = one_mesh(conduct, start_field, observed_mesh, apply_operator)
        grad_tiles = jnp.transpose(summed.reshape(N_SUB, CX, TILES, BY, CZ), (0, 2, 1, 3, 4))
        carry = carry.at[:, block_ids].add(grad_tiles)
        return carry, final_field

    gradient, last_field = lax.scan(per_mesh, jnp.zeros_like(conductivity), (footprint, initial, observed))
    return (gradient, last_field)
```

```python
import functools

import jax
import jax.numpy as jnp
from jax import lax
from jax.experimental import pallas as pl
from jax.experimental.pallas import tpu as pltpu
from jax.sharding import PartitionSpec as P

STEPS = 3
DEG = 6
LOW = 0.3
HIGH = 15.0
CENTRE = (HIGH + LOW) / 2.0
HALF = (HIGH - LOW) / 2.0
HALO = 40
UNIT = 16
OFF = 56


def weights():
    rho = HALF / CENTRE
    out = []
    for _ in range(DEG):
        new = 1.0 / (2.0 * CENTRE / HALF - rho)
        out.append((new * rho, 2.0 * new / HALF))
        rho = new
    return out


def beside(ref, p, r):
    nx, _, nz = p.shape
    zero = jnp.zeros((1,) + p.shape[1:], p.dtype)
    lane = lax.broadcasted_iota(jnp.int32, p.shape, 2)
    left = jnp.where(lane == 0, 0.0, pltpu.roll(p, 1, 2))
    right = jnp.where(lane == nz - 1, 0.0, pltpu.roll(p, nz - 1, 2))
    total = ref[:, pl.ds(r - 1, UNIT), :] + ref[:, pl.ds(r + 1, UNIT), :]
    total = total + (left + right)
    total = total + jnp.concatenate([zero, p[:-1]], axis=0)
    return total + jnp.concatenate([p[1:], zero], axis=0)


def evolve(rows, sub, n_sub, cond, u0, obs, src, even, odd, us, adj, grad):
    total_apps = 2 * STEPS * DEG
    first = sub == 0
    last = sub == n_sub - 1

    def sweep(app, fn):
        units = -(-(total_apps - app) // UNIT)
        lo = jnp.where(first, 0, -units)
        hi = jnp.where(last, 0, units) + rows // UNIT

        def step(i, carry):
            fn(pl.multiple_of(OFF + i * UNIT, 8))
            return carry

        lax.fori_loop(lo, hi, step, 0)

    def at(ref, r):
        return ref[:, pl.ds(r, UNIT), :]

    def put(ref, r, value):
        ref[:, pl.ds(r, UNIT), :] = value

    def start(r):
        put(src, r, at(cond, r) * at(u0, r))

    sweep(0, start)
    fields = [u0] + list(us)
    w = weights()
    app = 0
    for solve in range(2 * STEPS):
        for k in range(DEG):
            app += 1
            a, b = w[k]

            def one(r, k=k, a=a, b=b, solve=solve):
                c = at(cond, r)
                if k == 0:
                    s = at(src, r)
                    mul = (1.0 + a - 6.0 * b) / CENTRE + b
                    put(even, r, (mul - (b / CENTRE) * c) * s + (b / CENTRE) * beside(src, s, r))
                    return
                here, there = (even, odd) if k % 2 == 1 else (odd, even)
                p = at(here, r)
                s = at(src, r)
                acc = beside(here, p, r) + s + (((1.0 + a) / b - 6.0) - c) * p
                if k == 1:
                    new = b * acc - (a / CENTRE) * s
                else:
                    new = b * acc - a * at(there, r)
                if k < DEG - 1:
                    put(there, r, new)
                    return
                if solve < STEPS:
                    put(fields[solve + 1], r, new)
                    if solve < STEPS - 1:
                        put(src, r, c * new)
                    else:
                        put(src, r, new - obs[STEPS - 1, :, pl.ds(r, UNIT), :])
                    return
                n = 2 * STEPS - solve
                older = at(fields[n - 1], r)
                add = new * (older - at(fields[n], r))
                if n == STEPS:
                    put(grad, r, add)
                else:
                    put(grad, r, at(grad, r) + add)
                if n > 1:
                    put(src, r, older - obs[n - 2, :, pl.ds(r, UNIT), :] + c * new)

            sweep(app, one)


def choose(x, ids):
    rows = [lax.dynamic_index_in_dim(x, ids[i], 0, keepdims=True) for i in range(ids.shape[0])]
    return jnp.concatenate(rows, axis=0)


def local_kernel(n_sub, rows, c_ref, u_ref, o_ref, last_ref, g_ref, cond, u0, obs, src, even, odd, u1, u2, u3, grad):
    sub = lax.axis_index("sub")
    wide = rows + 2 * HALO
    for ref in (src, even, odd):
        ref[...] = jnp.zeros_like(ref)
    window = pl.ds(OFF - HALO, wide)
    cond[:, window, :] = c_ref[...]
    u0[:, window, :] = u_ref[...]
    obs[:, :, window, :] = o_ref[...]
    evolve(rows, sub, n_sub, cond, u0, obs, src, even, odd, (u1, u2, u3), None, grad)
    last_ref[...] = u3[:, pl.ds(OFF, rows), :]
    g_ref[...] = grad[:, pl.ds(OFF, rows), :]


def body(conductivity, footprint, initial, observed):
    n_mesh = lax.axis_size("mesh")
    n_sub = lax.axis_size("sub")
    me = lax.axis_index("mesh")
    _, per_owner, depth, block_y, nz = conductivity.shape
    tiles = footprint.shape[1]
    ny = tiles * block_y
    rows = ny // n_sub
    nx = depth * n_sub

    owners = footprint // per_owner
    local = footprint % per_owner
    mine = owners == me
    wanted = jnp.sum(jnp.where(mine, local, 0), axis=1)
    has = jnp.any(mine, axis=1)
    send = choose(conductivity[0], wanted)
    got = lax.all_to_all(send, "mesh", 0, 0, tiled=True)
    my_owners = lax.dynamic_index_in_dim(owners, me, 0, keepdims=False)
    picked = choose(got, my_owners)
    cond = jnp.transpose(picked, (1, 0, 2, 3)).reshape(depth, ny, nz)

    def spread(x):
        pads = [(0, 0)] * (x.ndim - 2) + [(HALO, HALO), (0, 0)]
        x = jnp.pad(x, pads)
        parts = [lax.slice_in_dim(x, s * rows, (s + 1) * rows + 2 * HALO, axis=x.ndim - 2) for s in range(n_sub)]
        y = lax.all_to_all(jnp.stack(parts), "sub", 0, 0, tiled=True)
        y = jnp.moveaxis(y, 0, -4)
        return y.reshape(y.shape[:-4] + (nx,) + y.shape[-2:])

    o = spread(observed[0])
    cu = spread(jnp.stack([cond, initial[0]]))

    full = pltpu.VMEM((nx, rows + 2 * OFF, nz), jnp.float32)
    vm = pl.BlockSpec(memory_space=pltpu.VMEM)
    out = jax.ShapeDtypeStruct((nx, rows, nz), jnp.float32)
    final, grad = pl.pallas_call(
        functools.partial(local_kernel, n_sub, rows),
        out_shape=(out, out),
        in_specs=[vm] * 3,
        out_specs=(vm, vm),
        scratch_shapes=[full, full, pltpu.VMEM((STEPS, nx, rows + 2 * OFF, nz), jnp.float32)] + [full] * 7,
        compiler_params=pltpu.CompilerParams(vmem_limit_bytes=48 * 1024 * 1024),
    )(cu[0], cu[1], o)

    def collect(x):
        y = lax.all_to_all(x, "sub", 0, 0, tiled=True)
        y = y.reshape(n_sub, depth, rows, nz)
        return jnp.transpose(y, (1, 0, 2, 3)).reshape(depth, ny, nz)

    g = collect(grad)
    final_field = collect(final)
    g_tiles = jnp.transpose(g.reshape(depth, tiles, block_y, nz), (1, 0, 2, 3))
    hit = my_owners[None, :] == jnp.arange(n_mesh, dtype=jnp.int32)[:, None]
    which = jnp.sum(jnp.where(hit, jnp.arange(tiles, dtype=jnp.int32)[None, :], 0), axis=1)
    back = lax.all_to_all(choose(g_tiles, which), "mesh", 0, 0, tiled=True)
    keep = (wanted[None, :] == jnp.arange(per_owner, dtype=jnp.int32)[:, None]) & has[None, :]
    gradient = jnp.sum(jnp.where(keep[:, :, None, None, None], back[None], 0.0), axis=1)
    return gradient[None], final_field[None]


def solution(mesh):
    return jax.shard_map(
        body,
        mesh=mesh,
        in_specs=(
            P("sub", "mesh", None, None, None),
            P(),
            P("mesh", "sub", None, None),
            P("mesh", None, "sub", None, None),
        ),
        out_specs=(P("sub", "mesh", None, None, None), P("mesh", "sub", None, None)),
        check_vma=False,
    )
```

```python
import functools

import jax
import jax.numpy as jnp
from jax import lax
from jax.experimental import pallas as pl
from jax.experimental.pallas import tpu as pltpu
from jax.sharding import PartitionSpec as P

STEPS = 3
DEG = 6
LOW = 0.3
HIGH = 15.0
CENTRE = (HIGH + LOW) / 2.0
HALF = (HIGH - LOW) / 2.0
HALO = 40
UNIT = 16
MESH = pl.DeviceIdType.MESH
OFF = 88


def weights():
    rho = HALF / CENTRE
    out = []
    for _ in range(DEG):
        new = 1.0 / (2.0 * CENTRE / HALF - rho)
        out.append((new * rho, 2.0 * new / HALF))
        rho = new
    return out


def beside(ref, p, r):
    nx, _, nz = p.shape
    zero = jnp.zeros((1,) + p.shape[1:], p.dtype)
    lane = lax.broadcasted_iota(jnp.int32, p.shape, 2)
    left = jnp.where(lane == 0, 0.0, pltpu.roll(p, 1, 2))
    right = jnp.where(lane == nz - 1, 0.0, pltpu.roll(p, nz - 1, 2))
    total = ref[:, pl.ds(r - 1, UNIT), :] + ref[:, pl.ds(r + 1, UNIT), :]
    total = total + (left + right)
    total = total + jnp.concatenate([zero, p[:-1]], axis=0)
    return total + jnp.concatenate([p[1:], zero], axis=0)


def evolve(rows, sub, n_sub, cond, u0, obs, src, even, odd, us, grad, need_obs, forward_done):
    total_apps = 2 * STEPS * DEG
    first = sub == 0
    last = sub == n_sub - 1

    def sweep(app, fn):
        units = -(-(total_apps - app) // UNIT)
        lo = jnp.where(first, 0, -units)
        hi = jnp.where(last, 0, units) + rows // UNIT

        def step(i, carry):
            fn(pl.multiple_of(OFF + i * UNIT, 8))
            return carry

        lax.fori_loop(lo, hi, step, 0)

    def at(ref, r):
        return ref[:, pl.ds(r, UNIT), :]

    def put(ref, r, value):
        ref[:, pl.ds(r, UNIT), :] = value

    def start(r):
        put(src, r, at(cond, r) * at(u0, r))

    sweep(0, start)
    fields = [u0] + list(us)
    w = weights()
    app = 0
    for solve in range(2 * STEPS):
        for k in range(DEG):
            app += 1
            a, b = w[k]

            def one(r, k=k, a=a, b=b, solve=solve):
                c = at(cond, r)
                if k == 0:
                    s = at(src, r)
                    mul = (1.0 + a - 6.0 * b) / CENTRE + b
                    put(even, r, (mul - (b / CENTRE) * c) * s + (b / CENTRE) * beside(src, s, r))
                    return
                here, there = (even, odd) if k % 2 == 1 else (odd, even)
                p = at(here, r)
                s = at(src, r)
                acc = beside(here, p, r) + s + (((1.0 + a) / b - 6.0) - c) * p
                if k == 1:
                    new = b * acc - (a / CENTRE) * s
                else:
                    new = b * acc - a * at(there, r)
                if k < DEG - 1:
                    put(there, r, new)
                    return
                if solve < STEPS:
                    put(fields[solve + 1], r, new)
                    if solve < STEPS - 1:
                        put(src, r, c * new)
                    else:
                        put(src, r, new - obs[STEPS - 1, :, pl.ds(r, UNIT), :])
                    return
                n = 2 * STEPS - solve
                older = at(fields[n - 1], r)
                add = new * (older - at(fields[n], r))
                if n == STEPS:
                    put(grad, r, add)
                else:
                    put(grad, r, at(grad, r) + add)
                if n > 1:
                    put(src, r, older - obs[n - 2, :, pl.ds(r, UNIT), :] + c * new)

            if k == DEG - 1 and STEPS - 1 <= solve < 2 * STEPS - 1:
                need_obs(2 * STEPS - 2 - solve)
            sweep(app, one)
        if solve == STEPS - 1:
            forward_done()


def whole_kernel(n_mesh, n_sub, rows, foot, c_ref, u_ref, o_ref, grad_ref, last_ref, send_c, got_c, layer, cond, u0, obs,
                 src, even, odd, u1, u2, u3, grad, tiles_g, send_g, got_g,
                 mesh_send, mesh_recv, back_send, back_recv, sub_send, sub_recv, near):
    sub = lax.axis_index("sub")
    me = lax.axis_index("mesh")
    per_owner, depth, block_y, nz = c_ref.shape[1:]
    tiles = foot.shape[1]
    ny = tiles * block_y
    per_dev = tiles // n_sub
    f_u, f_c, f_last, f_g = STEPS, STEPS + 1, STEPS + 2, STEPS + 3

    barrier = pltpu.get_barrier_semaphore()
    for d in range(1, n_sub):
        pl.semaphore_signal(barrier, inc=1, device_id={"sub": lax.rem(sub + d, n_sub)}, device_id_type=MESH)
    for d in range(1, n_mesh):
        pl.semaphore_signal(barrier, inc=1, device_id={"mesh": lax.rem(me + d, n_mesh)}, device_id_type=MESH)

    base = me * per_owner
    slot, known, tile_of = [], [], []
    for d in range(n_mesh):
        m = lax.rem(me + d, n_mesh)
        pick = jnp.int32(0)
        has = jnp.int32(0)
        for t in range(tiles):
            rel = foot[m, t] - base
            inside = (rel >= 0) & (rel < per_owner)
            pick = jnp.where(inside, rel, pick)
            has = jnp.where(inside, 1, has)
        slot.append(pick)
        known.append(has)
        mine = jnp.int32(0)
        for t in range(tiles):
            rel = foot[me, t] - m * per_owner
            mine = jnp.where((rel >= 0) & (rel < per_owner), t, mine)
        tile_of.append(mine)

    pl.semaphore_wait(barrier, n_sub + n_mesh - 2)

    def mesh_copy(d, send, got, ss, rs):
        return pltpu.make_async_remote_copy(
            src_ref=send.at[d], dst_ref=got.at[me], send_sem=ss.at[d], recv_sem=rs.at[d],
            device_id={"mesh": lax.rem(me + d, n_mesh)}, device_id_type=MESH)

    out_c = []
    for d in range(1, n_mesh):
        send_c[d] = c_ref[0, slot[d]]
        out_c.append(mesh_copy(d, send_c, got_c, mesh_send, mesh_recv))
        out_c[-1].start()
    got_c[me] = c_ref[0, slot[0]]

    def spread(f, source, target, halo):
        wide = rows + 2 * halo
        copies = []
        for d in [1, 2, 3, 0] if n_sub == 4 else list(range(n_sub)):
            to = lax.rem(sub + d, n_sub)
            begin = jnp.clip(to * rows - halo, 0, ny - wide)
            begin = pl.multiple_of(begin, 8)
            land = pl.multiple_of(OFF + begin - to * rows, 8)
            from_ref = source.at[:, pl.ds(begin, wide), :]
            to_ref = target.at[pl.ds(depth * sub, depth), pl.ds(land, wide), :]
            if d == 0:
                copy = pltpu.make_async_copy(from_ref, to_ref, near.at[f])
            else:
                copy = pltpu.make_async_remote_copy(
                    src_ref=from_ref, dst_ref=to_ref, send_sem=sub_send.at[f, d], recv_sem=sub_recv.at[f, d],
                    device_id={"sub": to}, device_id_type=MESH)
            copy.start()
            copies.append((d, copy))
        return copies

    def arrive(copies):
        for d, copy in copies:
            if d == 0:
                copy.wait()
            else:
                copy.wait_recv()

    halos = [-(-(DEG * n) // 8) * 8 for n in range(1, STEPS + 1)]
    ready = {}
    ready["u"] = spread(f_u, u_ref.at[0], u0, HALO)
    ready[STEPS - 1] = spread(STEPS - 1, o_ref.at[0, STEPS - 1], obs.at[STEPS - 1], halos[STEPS - 1])

    for ref in (src, even, odd):
        ref[...] = jnp.zeros_like(ref)

    for copy in out_c:
        copy.wait_recv()
    for t in range(tiles):
        owner = lax.div(foot[me, t], jnp.int32(per_owner))
        layer[:, t * block_y:(t + 1) * block_y, :] = got_c[owner]
    ready["c"] = spread(f_c, layer, cond, HALO)
    for n in range(STEPS - 2, -1, -1):
        ready[n] = spread(n, o_ref.at[0, n], obs.at[n], halos[n])
    arrive(ready["u"])
    arrive(ready["c"])

    def forward_done():
        copies = []
        for d in range(n_sub):
            to = lax.rem(sub + d, n_sub)
            from_ref = u3.at[pl.ds(depth * to, depth), pl.ds(OFF, rows), :]
            to_ref = last_ref.at[0, :, pl.ds(sub * rows, rows), :]
            if d == 0:
                copy = pltpu.make_async_copy(from_ref, to_ref, near.at[f_last])
            else:
                copy = pltpu.make_async_remote_copy(
                    src_ref=from_ref, dst_ref=to_ref, send_sem=sub_send.at[f_last, d],
                    recv_sem=sub_recv.at[f_last, d], device_id={"sub": to}, device_id_type=MESH)
            copy.start()
            copies.append((d, copy))
        ready["last"] = copies

    evolve(rows, sub, n_sub, cond, u0, obs, src, even, odd, (u1, u2, u3), grad,
           lambda n: arrive(ready[n]), forward_done)

    copies = []
    for d in list(range(1, n_sub)) + [0]:
        to = lax.rem(sub + d, n_sub)
        for j in range(per_dev):
            from_ref = grad.at[pl.ds(depth * to, depth), pl.ds(OFF + j * block_y, block_y), :]
            to_ref = tiles_g.at[sub * per_dev + j]
            f = f_g + j
            if d == 0:
                copy = pltpu.make_async_copy(from_ref, to_ref, near.at[f])
            else:
                copy = pltpu.make_async_remote_copy(
                    src_ref=from_ref, dst_ref=to_ref, send_sem=sub_send.at[f, d], recv_sem=sub_recv.at[f, d],
                    device_id={"sub": to}, device_id_type=MESH)
            copy.start()
            copies.append((d, copy))
    ready["g"] = copies
    arrive(copies)

    out_g = []
    for d in range(1, n_mesh):
        send_g[d] = tiles_g[tile_of[d]]
        out_g.append(mesh_copy(d, send_g, got_g, back_send, back_recv))
        out_g[-1].start()
    got_g[me] = tiles_g[tile_of[0]]
    for copy in out_g:
        copy.wait_recv()
    for b in range(per_owner):
        total = jnp.zeros((depth, block_y, nz), jnp.float32)
        for d in range(n_mesh):
            use = (slot[d] == b) & (known[d] == 1)
            total = total + jnp.where(use, got_g[lax.rem(me + d, n_mesh)], 0.0)
        grad_ref[0, b] = total

    arrive(ready["last"])
    for copies in ready.values():
        for d, copy in copies:
            if d:
                copy.wait_send()
    for copy in out_c + out_g:
        copy.wait_send()


def body(conductivity, footprint, initial, observed):
    n_mesh = lax.axis_size("mesh")
    n_sub = lax.axis_size("sub")
    _, per_owner, depth, block_y, nz = conductivity.shape
    tiles = footprint.shape[1]
    ny = tiles * block_y
    rows = ny // n_sub
    nx = depth * n_sub
    per_dev = tiles // n_sub

    def vmem(*shape):
        return pltpu.VMEM(shape, jnp.float32)

    full = vmem(nx, rows + 2 * OFF, nz)
    blocks = vmem(n_mesh, depth, block_y, nz)
    dma = pltpu.SemaphoreType.DMA
    fields = STEPS + 3 + per_dev
    vm = pl.BlockSpec(memory_space=pltpu.VMEM)
    hbm = pl.BlockSpec(memory_space=pl.ANY)
    return pl.pallas_call(
        functools.partial(whole_kernel, n_mesh, n_sub, rows),
        out_shape=(
            jax.ShapeDtypeStruct(conductivity.shape, jnp.float32),
            jax.ShapeDtypeStruct(initial.shape, jnp.float32),
        ),
        in_specs=[pl.BlockSpec(memory_space=pltpu.SMEM), vm, hbm, hbm],
        out_specs=(vm, hbm),
        scratch_shapes=[blocks, blocks, vmem(depth, ny, nz), full, full, vmem(STEPS, nx, rows + 2 * OFF, nz)]
        + [full] * 7
        + [vmem(tiles, depth, block_y, nz), blocks, blocks]
        + [dma((n_mesh,))] * 4
        + [dma((fields, n_sub))] * 2
        + [dma((fields,))],
        compiler_params=pltpu.CompilerParams(
            collective_id=0, has_side_effects=True, vmem_limit_bytes=48 * 1024 * 1024
        ),
    )(footprint, conductivity, initial, observed)


def solution(mesh):
    return jax.shard_map(
        body,
        mesh=mesh,
        in_specs=(
            P("sub", "mesh", None, None, None),
            P(),
            P("mesh", "sub", None, None),
            P("mesh", None, "sub", None, None),
        ),
        out_specs=(P("sub", "mesh", None, None, None), P("mesh", "sub", None, None)),
        check_vma=False,
    )
```

```python
import functools

import jax
import jax.numpy as jnp
from jax import lax
from jax.experimental import pallas as pl
from jax.experimental.pallas import tpu as pltpu
from jax.sharding import PartitionSpec as P

STEPS = 3
DEG = 6
LOW = 0.3
HIGH = 15.0
CENTRE = (HIGH + LOW) / 2.0
HALF = (HIGH - LOW) / 2.0
HALO = 40
UNIT = 104
MESH = pl.DeviceIdType.MESH
OFF = 88


def weights():
    rho = HALF / CENTRE
    out = []
    for _ in range(DEG):
        new = 1.0 / (2.0 * CENTRE / HALF - rho)
        out.append((new * rho, 2.0 * new / HALF))
        rho = new
    return out


def beside(ref, p, r):
    nx, _, nz = p.shape
    zero = jnp.zeros((1,) + p.shape[1:], p.dtype)
    lane = lax.broadcasted_iota(jnp.int32, p.shape, 2)
    left = jnp.where(lane == 0, 0.0, pltpu.roll(p, 1, 2))
    right = jnp.where(lane == nz - 1, 0.0, pltpu.roll(p, nz - 1, 2))
    total = ref[:, pl.ds(r - 1, p.shape[1]), :] + ref[:, pl.ds(r + 1, p.shape[1]), :]
    total = total + (left + right)
    total = total + jnp.concatenate([zero, p[:-1]], axis=0)
    return total + jnp.concatenate([p[1:], zero], axis=0)


def evolve(rows, sub, n_sub, cond, u0, obs, src, even, odd, us, grad, need_obs, forward_done):
    total_apps = 2 * STEPS * DEG
    first = sub == 0
    last = sub == n_sub - 1

    def sweep(app, fn):
        halo = -(-(total_apps - app) // 8) * 8
        count = rows + 2 * halo
        begin = OFF - jnp.where(first, 0, jnp.where(last, 2 * halo, halo))
        whole, rest = divmod(count, UNIT)

        def step(i, carry):
            fn(pl.multiple_of(begin + i * UNIT, 8), UNIT)
            return carry

        lax.fori_loop(0, whole, step, 0)
        if rest:
            fn(pl.multiple_of(begin + whole * UNIT, 8), rest)

    def put(ref, r, value):
        ref[:, pl.ds(r, value.shape[1]), :] = value

    def start(r, size):
        part = pl.ds(r, size)
        put(src, r, cond[:, part, :] * u0[:, part, :])

    sweep(0, start)
    fields = [u0] + list(us)
    w = weights()
    app = 0
    for solve in range(2 * STEPS):
        for k in range(DEG):
            app += 1
            a, b = w[k]

            def one(r, size, k=k, a=a, b=b, solve=solve):
                at = lambda ref, r: ref[:, pl.ds(r, size), :]
                c = at(cond, r)
                if k == 0:
                    s = at(src, r)
                    mul = (1.0 + a - 6.0 * b) / CENTRE + b
                    put(even, r, (mul - (b / CENTRE) * c) * s + (b / CENTRE) * beside(src, s, r))
                    return
                here, there = (even, odd) if k % 2 == 1 else (odd, even)
                p = at(here, r)
                s = at(src, r)
                acc = beside(here, p, r) + s + (((1.0 + a) / b - 6.0) - c) * p
                if k == 1:
                    new = b * acc - (a / CENTRE) * s
                else:
                    new = b * acc - a * at(there, r)
                if k < DEG - 1:
                    put(there, r, new)
                    return
                if solve < STEPS:
                    put(fields[solve + 1], r, new)
                    if solve < STEPS - 1:
                        put(src, r, c * new)
                    else:
                        put(src, r, new - obs[STEPS - 1, :, pl.ds(r, size), :])
                    return
                n = 2 * STEPS - solve
                older = at(fields[n - 1], r)
                add = new * (older - at(fields[n], r))
                if n == STEPS:
                    put(grad, r, add)
                else:
                    put(grad, r, at(grad, r) + add)
                if n > 1:
                    put(src, r, older - obs[n - 2, :, pl.ds(r, size), :] + c * new)

            if k == DEG - 1 and STEPS - 1 <= solve < 2 * STEPS - 1:
                need_obs(2 * STEPS - 2 - solve)
            sweep(app, one)
        if solve == STEPS - 1:
            forward_done()


def whole_kernel(n_mesh, n_sub, rows, foot, c_ref, u_ref, o_ref, grad_ref, last_ref, send_c, got_c, layer, cond, u0, obs,
                 src, even, odd, u1, u2, u3, grad, tiles_g, send_g, got_g,
                 mesh_send, mesh_recv, back_send, back_recv, sub_send, sub_recv, near):
    sub = lax.axis_index("sub")
    me = lax.axis_index("mesh")
    per_owner, depth, block_y, nz = c_ref.shape[1:]
    tiles = foot.shape[1]
    ny = tiles * block_y
    per_dev = tiles // n_sub
    f_u, f_c, f_last, f_g = STEPS, STEPS + 1, STEPS + 2, STEPS + 3

    barrier = pltpu.get_barrier_semaphore()
    for d in range(1, n_sub):
        pl.semaphore_signal(barrier, inc=1, device_id={"sub": lax.rem(sub + d, n_sub)}, device_id_type=MESH)
    for d in range(1, n_mesh):
        pl.semaphore_signal(barrier, inc=1, device_id={"mesh": lax.rem(me + d, n_mesh)}, device_id_type=MESH)

    base = me * per_owner
    slot, known, tile_of = [], [], []
    for d in range(n_mesh):
        m = lax.rem(me + d, n_mesh)
        pick = jnp.int32(0)
        has = jnp.int32(0)
        for t in range(tiles):
            rel = foot[m, t] - base
            inside = (rel >= 0) & (rel < per_owner)
            pick = jnp.where(inside, rel, pick)
            has = jnp.where(inside, 1, has)
        slot.append(pick)
        known.append(has)
        mine = jnp.int32(0)
        for t in range(tiles):
            rel = foot[me, t] - m * per_owner
            mine = jnp.where((rel >= 0) & (rel < per_owner), t, mine)
        tile_of.append(mine)

    pl.semaphore_wait(barrier, n_sub + n_mesh - 2)

    def mesh_copy(d, send, got, ss, rs):
        return pltpu.make_async_remote_copy(
            src_ref=send.at[d], dst_ref=got.at[me], send_sem=ss.at[d], recv_sem=rs.at[d],
            device_id={"mesh": lax.rem(me + d, n_mesh)}, device_id_type=MESH)

    out_c = []
    for d in range(1, n_mesh):
        send_c[d] = c_ref[0, slot[d]]
        out_c.append(mesh_copy(d, send_c, got_c, mesh_send, mesh_recv))
        out_c[-1].start()
    got_c[me] = c_ref[0, slot[0]]

    def spread(f, source, target, halo):
        wide = rows + 2 * halo
        copies = []
        for d in [1, 2, 3, 0] if n_sub == 4 else list(range(n_sub)):
            to = lax.rem(sub + d, n_sub)
            begin = jnp.clip(to * rows - halo, 0, ny - wide)
            begin = pl.multiple_of(begin, 8)
            land = pl.multiple_of(OFF + begin - to * rows, 8)
            from_ref = source.at[:, pl.ds(begin, wide), :]
            to_ref = target.at[pl.ds(depth * sub, depth), pl.ds(land, wide), :]
            if d == 0:
                copy = pltpu.make_async_copy(from_ref, to_ref, near.at[f])
            else:
                copy = pltpu.make_async_remote_copy(
                    src_ref=from_ref, dst_ref=to_ref, send_sem=sub_send.at[f, d], recv_sem=sub_recv.at[f, d],
                    device_id={"sub": to}, device_id_type=MESH)
            copy.start()
            copies.append((d, copy))
        return copies

    def arrive(copies):
        for d, copy in copies:
            if d == 0:
                copy.wait()
            else:
                copy.wait_recv()

    halos = [-(-(DEG * n) // 8) * 8 for n in range(1, STEPS + 1)]
    ready = {}
    ready["u"] = spread(f_u, u_ref.at[0], u0, HALO)
    ready[STEPS - 1] = spread(STEPS - 1, o_ref.at[0, STEPS - 1], obs.at[STEPS - 1], halos[STEPS - 1])

    for ref in (src, even, odd):
        ref[...] = jnp.zeros_like(ref)

    for copy in out_c:
        copy.wait_recv()
    for t in range(tiles):
        owner = lax.div(foot[me, t], jnp.int32(per_owner))
        layer[:, t * block_y:(t + 1) * block_y, :] = got_c[owner]
    ready["c"] = spread(f_c, layer, cond, HALO)
    for n in range(STEPS - 2, -1, -1):
        ready[n] = spread(n, o_ref.at[0, n], obs.at[n], halos[n])
    arrive(ready["u"])
    arrive(ready["c"])

    def forward_done():
        copies = []
        for d in range(n_sub):
            to = lax.rem(sub + d, n_sub)
            from_ref = u3.at[pl.ds(depth * to, depth), pl.ds(OFF, rows), :]
            to_ref = last_ref.at[0, :, pl.ds(sub * rows, rows), :]
            if d == 0:
                copy = pltpu.make_async_copy(from_ref, to_ref, near.at[f_last])
            else:
                copy = pltpu.make_async_remote_copy(
                    src_ref=from_ref, dst_ref=to_ref, send_sem=sub_send.at[f_last, d],
                    recv_sem=sub_recv.at[f_last, d], device_id={"sub": to}, device_id_type=MESH)
            copy.start()
            copies.append((d, copy))
        ready["last"] = copies

    evolve(rows, sub, n_sub, cond, u0, obs, src, even, odd, (u1, u2, u3), grad,
           lambda n: arrive(ready[n]), forward_done)

    copies = []
    for d in list(range(1, n_sub)) + [0]:
        to = lax.rem(sub + d, n_sub)
        for j in range(per_dev):
            from_ref = grad.at[pl.ds(depth * to, depth), pl.ds(OFF + j * block_y, block_y), :]
            to_ref = tiles_g.at[sub * per_dev + j]
            f = f_g + j
            if d == 0:
                copy = pltpu.make_async_copy(from_ref, to_ref, near.at[f])
            else:
                copy = pltpu.make_async_remote_copy(
                    src_ref=from_ref, dst_ref=to_ref, send_sem=sub_send.at[f, d], recv_sem=sub_recv.at[f, d],
                    device_id={"sub": to}, device_id_type=MESH)
            copy.start()
            copies.append((d, copy))
    ready["g"] = copies
    arrive(copies)

    out_g = []
    for d in range(1, n_mesh):
        send_g[d] = tiles_g[tile_of[d]]
        out_g.append(mesh_copy(d, send_g, got_g, back_send, back_recv))
        out_g[-1].start()
    got_g[me] = tiles_g[tile_of[0]]
    for copy in out_g:
        copy.wait_recv()
    for b in range(per_owner):
        total = jnp.zeros((depth, block_y, nz), jnp.float32)
        for d in range(n_mesh):
            use = (slot[d] == b) & (known[d] == 1)
            total = total + jnp.where(use, got_g[lax.rem(me + d, n_mesh)], 0.0)
        grad_ref[0, b] = total

    arrive(ready["last"])
    for copies in ready.values():
        for d, copy in copies:
            if d:
                copy.wait_send()
    for copy in out_c + out_g:
        copy.wait_send()


def body(conductivity, footprint, initial, observed):
    n_mesh = lax.axis_size("mesh")
    n_sub = lax.axis_size("sub")
    _, per_owner, depth, block_y, nz = conductivity.shape
    tiles = footprint.shape[1]
    ny = tiles * block_y
    rows = ny // n_sub
    nx = depth * n_sub
    per_dev = tiles // n_sub

    def vmem(*shape):
        return pltpu.VMEM(shape, jnp.float32)

    full = vmem(nx, rows + 2 * OFF, nz)
    blocks = vmem(n_mesh, depth, block_y, nz)
    dma = pltpu.SemaphoreType.DMA
    fields = STEPS + 3 + per_dev
    vm = pl.BlockSpec(memory_space=pltpu.VMEM)
    hbm = pl.BlockSpec(memory_space=pl.ANY)
    return pl.pallas_call(
        functools.partial(whole_kernel, n_mesh, n_sub, rows),
        out_shape=(
            jax.ShapeDtypeStruct(conductivity.shape, jnp.float32),
            jax.ShapeDtypeStruct(initial.shape, jnp.float32),
        ),
        in_specs=[pl.BlockSpec(memory_space=pltpu.SMEM), vm, hbm, hbm],
        out_specs=(vm, hbm),
        scratch_shapes=[blocks, blocks, vmem(depth, ny, nz), full, full, vmem(STEPS, nx, rows + 2 * OFF, nz)]
        + [full] * 7
        + [vmem(tiles, depth, block_y, nz), blocks, blocks]
        + [dma((n_mesh,))] * 4
        + [dma((fields, n_sub))] * 2
        + [dma((fields,))],
        compiler_params=pltpu.CompilerParams(
            collective_id=0, has_side_effects=True, vmem_limit_bytes=48 * 1024 * 1024
        ),
    )(footprint, conductivity, initial, observed)


def solution(mesh):
    return jax.shard_map(
        body,
        mesh=mesh,
        in_specs=(
            P("sub", "mesh", None, None, None),
            P(),
            P("mesh", "sub", None, None),
            P("mesh", None, "sub", None, None),
        ),
        out_specs=(P("sub", "mesh", None, None, None), P("mesh", "sub", None, None)),
        check_vma=False,
    )
```
